32 devices in a mesh: dp: 8 (over z, x), tensor: 4 (over y, core).
Axes of the slice: x: 2, y: 2, z: 4, core: 2. Of those that a mesh axis runs over, the one named last changes fastest.
Arguments:
- hidden_in: bfloat16 [8192, 1024], P(('dp', 'tensor')), may hold values from -6 to 6
- out_grad: bfloat16 [8192, 1024], P(('dp', 'tensor')), may hold values from -6 to 6
- seq_lengths: int32 [8], P('dp'), may hold values from 256 to 1024, as said below
- norm1_gain: float32 [1024], replicated, may hold values from 0.5 to 1.5
- zx_weight: bfloat16 [1024, 2, 1536], P(None, None, 'tensor'), may hold values from -0.1875 to 0.1875
- bc_weight: bfloat16 [1024, 256], replicated, may hold values from -0.1875 to 0.1875
- dt_weight: bfloat16 [1024, 24], P(None, 'tensor'), may hold values from -0.1875 to 0.1875
- convx_weight: float32 [4, 1536], P(None, 'tensor'), may hold values from -3 to 3
- convx_bias: float32 [1536], P('tensor'), may hold values from -0.5 to 0.5
- convbc_weight: float32 [4, 256], replicated, may hold values from -3 to 3
- convbc_bias: float32 [256], replicated, may hold values from -0.5 to 0.5
- dt_bias: float32 [24], P('tensor'), may hold values from -6 to -2.5
- a_log: float32 [24], P('tensor'), may hold values from 0 to 2.77
- d_skip: float32 [24], P('tensor'), may hold values from 0.5 to 1.5
- mnorm_gain: float32 [1536], P('tensor'), may hold values from 0.5 to 1.5
- mo_weight: bfloat16 [1536, 1024], P('tensor'), may hold values from -0.15625 to 0.15625
- q_weight: bfloat16 [1024, 512], P(None, 'tensor'), may hold values from -0.1875 to 0.1875
- kv_weight: bfloat16 [1024, 2, 128], replicated, may hold values from -0.1875 to 0.1875
- o_weight: bfloat16 [512, 1024], P('tensor'), may hold values from -6 to 6
- norm2_gain: float32 [1024], replicated, may hold values from 0.5 to 1.5
- gu_weight: bfloat16 [1024, 2, 2048], P(None, None, 'tensor'), may hold values from -0.1875 to 0.1875
- down_weight: bfloat16 [2048, 1024], P('tensor'), may hold values from -0.125 to 0.125
Outputs:
- hidden_out: float32 [8192, 1024], P(('dp', 'tensor'))
- hidden_grad: float32 [8192, 1024], P(('dp', 'tensor'))
- grad_norm1_gain: float32 [1024], replicated
- grad_zx_weight: float32 [1024, 2, 1536], P(None, None, 'tensor')
- grad_bc_weight: float32 [1024, 256], replicated
- grad_dt_weight: float32 [1024, 24], P(None, 'tensor')
- grad_convx_weight: float32 [4, 1536], P(None, 'tensor')
- grad_convx_bias: float32 [1536], P('tensor')
- grad_convbc_weight: float32 [4, 256], replicated
- grad_convbc_bias: float32 [256], replicated
- grad_dt_bias: float32 [24], P('tensor')
- grad_a_log: float32 [24], P('tensor')
- grad_d_skip: float32 [24], P('tensor')
- grad_mnorm_gain: float32 [1536], P('tensor')
- grad_mo_weight: float32 [1536, 1024], P('tensor')
- grad_q_weight: float32 [1024, 512], P(None, 'tensor')
- grad_kv_weight: float32 [1024, 2, 128], replicated
- grad_o_weight: float32 [512, 1024], P('tensor')
- grad_norm2_gain: float32 [1024], replicated
- grad_gu_weight: float32 [1024, 2, 2048], P(None, None, 'tensor')
- grad_down_weight: float32 [2048, 1024], P('tensor')
The draws below stay inside these ranges and needn't reach their ends.
Inputs may be any that keep to these rules, and one draw needn't show every extreme that they name: Each sequence's live rows are the first seq_lengths rows of its slot of 1024 rows; some sequence is 1024 long in every draw.
All inputs are finite; a program needn't handle non-finite values.
Results may differ from the reference program's by a relative error of at most 0.02.
Values may be sent and summed in bfloat16 or wider, within the bound.
A program may use at most 128 MiB of HBM per device.

```python
import jax
import jax.numpy as jnp
from jax import lax

D = 1024
MH = 24
NS = 128
KC = 4
QH = 8
KVH = 2
HD = 64
FF = 2048
LEN = 1024
DI = 1536
NSEQ = 8
TOKENS = 8192


def draw_seq_lengths(key, part):
    key = jax.random.fold_in(key, 7)
    first_key, second_key = jax.random.split(key)
    drawn = jax.random.randint(first_key, (NSEQ,), LEN // 4, LEN + 1)
    chosen = jax.random.randint(second_key, (), 0, NSEQ)
    return jnp.where(jnp.arange(NSEQ) == chosen, LEN, drawn).astype(jnp.int32)


def levels(key, shape, cuts, smallest, top_value):
    factor_of, own = 1.0, jax.random.fold_in(key, 6)
    for axis_at, blocks in cuts:
        draws = jnp.exp(jax.random.uniform(jax.random.fold_in(own, axis_at), (blocks,), jnp.float32, smallest / len(cuts), top_value / len(cuts)))
        factor_of = factor_of * jnp.repeat(draws, shape[axis_at] // blocks).reshape([-1 if axis == axis_at else 1 for axis in range(len(shape))])
    return factor_of


def normal_values(rng, extent, deviation, most, pieces=(), kind=jnp.bfloat16):
    result = jax.random.normal(rng, extent, jnp.float32) * deviation
    if len(pieces) > 0:
        result = levels(rng, extent, pieces, -0.22, 0.18) * result
    return jnp.clip(result, min=-most, max=most).astype(kind)


def setup_inputs(seed: int = 0) -> dict:
    streams_of = jax.random.split(jax.random.key(seed), 23)
    return {
        "hidden_in": normal_values(streams_of[0], (TOKENS, D), 1.0, 6.0, ((0, 32),)),
        "out_grad": normal_values(streams_of[1], (TOKENS, D), 1.0, 6.0, ((0, 32),)),
        "seq_lengths": draw_seq_lengths(jax.random.fold_in(streams_of[22], 71), 0),
        "norm1_gain": jnp.clip(1.0 + 0.1 * jax.random.normal(streams_of[3], (D,), jnp.float32), 0.5, 1.5),
        "zx_weight": normal_values(streams_of[4], (D, 2, DI), D ** -0.5, 0.1875, ((2, 4),)),
        "bc_weight": normal_values(streams_of[5], (D, 2 * NS), D ** -0.5, 0.1875),
        "dt_weight": normal_values(streams_of[6], (D, MH), D ** -0.5, 0.1875, ((1, 4),)),
        "convx_weight": normal_values(streams_of[7], (KC, DI), KC ** -0.5, 3.0, ((1, 4),), jnp.float32),
        "convx_bias": jnp.clip(jax.random.uniform(streams_of[8], (DI,), jnp.float32, -0.5, 0.5) * levels(streams_of[8], (DI,), ((0, 4),), -0.4, 0.0), -0.5, 0.5),
        "convbc_weight": normal_values(streams_of[9], (KC, 2 * NS), KC ** -0.5, 3.0, (), jnp.float32),
        "convbc_bias": jnp.clip(jax.random.uniform(streams_of[10], (2 * NS,), jnp.float32, -0.5, 0.5), -0.5, 0.5),
        "dt_bias": jnp.clip(-6.0 + 3.5 * jax.random.uniform(streams_of[11], (MH,), jnp.float32) ** levels(streams_of[11], (MH,), ((0, 4),), -0.2, 0.2), -6.0, -2.5),
        "a_log": jnp.clip(2.77 * jax.random.uniform(streams_of[12], (MH,), jnp.float32) ** levels(streams_of[12], (MH,), ((0, 4),), -0.2, 0.2), 0.0, 2.77),
        "d_skip": jnp.clip(0.5 + 1.0 * jax.random.uniform(streams_of[13], (MH,), jnp.float32) ** levels(streams_of[13], (MH,), ((0, 4),), -0.2, 0.2), 0.5, 1.5),
        "mnorm_gain": jnp.clip(1.0 + 0.1 * jax.random.normal(streams_of[14], (DI,), jnp.float32), 0.5, 1.5),
        "mo_weight": normal_values(streams_of[15], (DI, D), DI ** -0.5, 0.15625, ((0, 4),)),
        "q_weight": normal_values(streams_of[16], (D, QH * HD), D ** -0.5, 0.1875, ((1, 4),)),
        "kv_weight": normal_values(streams_of[17], (D, 2, KVH * HD), D ** -0.5, 0.1875),
        "o_weight": normal_values(streams_of[18], (QH * HD, D), (max(1, QH * HD * 2 // LEN)) ** -0.5, 6.0, ((0, 4),)),
        "norm2_gain": jnp.clip(1.0 + 0.1 * jax.random.normal(streams_of[19], (D,), jnp.float32), 0.5, 1.5),
        "gu_weight": normal_values(streams_of[20], (D, 2, FF), D ** -0.5, 0.1875, ((2, 4),)),
        "down_weight": normal_values(streams_of[21], (FF, D), FF ** -0.5, 0.125, ((0, 4),)),
    }


@jax.custom_vjp
def low(v):
    return lax.optimization_barrier(v.astype(jnp.bfloat16)).astype(jnp.float32)

@jax.custom_vjp
def low_back(v):
    return v

def low_keep(v):
    return (low(v), None)

def low_pass(kept, grad):
    return (grad,)

def back_keep(v):
    return (v, None)

def back_low(kept, grad):
    return (low(grad),)
low.defvjp(low_keep, low_pass)
low_back.defvjp(back_keep, back_low)
precise = lax.Precision.HIGHEST
epsilon = 1e-05

def matmul(left, right):
    return jnp.dot(left, right, precision=precise)

def contract_heads(form, left, right):
    return jnp.einsum(form, left, right, precision=precise)

def rms_scale(row_block, gain_vector):
    return row_block * lax.rsqrt(lax.optimization_barrier(jnp.mean(row_block * row_block, axis=-1, keepdims=True)) + epsilon) * gain_vector

def causal_conv(values, kernel, shift_bias):
    tap_count = kernel.shape[0]
    row_count = values.shape[0]
    padded = jnp.pad(values, ((tap_count - 1, 0), (0, 0)))
    summed = jnp.zeros_like(values) + shift_bias
    for offset in range(tap_count):
        summed = summed + kernel[offset] * padded[offset:offset + row_count]
    return summed

def rotate(values, head_count, head_dimension):
    row_count = values.shape[0]
    half_size = head_dimension // 2
    frequency = 10000.0 ** (-2.0 * jnp.arange(half_size, dtype=jnp.float32) / head_dimension)
    angles = jnp.arange(row_count, dtype=jnp.float32)[:, None] * frequency[None, :]
    cosine = jnp.cos(angles)[:, None, :]
    sine_part = jnp.sin(angles)[:, None, :]
    by_head = values.reshape(row_count, head_count, head_dimension)
    front_half = by_head[..., :half_size]
    back_half = by_head[..., half_size:]
    turned = jnp.concatenate([front_half * cosine - back_half * sine_part, back_half * cosine + front_half * sine_part], axis=-1)
    return turned.reshape(row_count, head_count * head_dimension)

def mamba_front(seq_rows, zx_weight, bc_weight, dt_weight, convx_weight, convx_bias, convbc_weight, convbc_bias, dt_bias, a_log, d_skip):
    row_count, model_width = seq_rows.shape
    inner_width = convx_weight.shape[1]
    head_count = dt_weight.shape[1]
    head_dimension = inner_width // head_count
    state_size = bc_weight.shape[1] // 2
    projected = low_back(matmul(seq_rows, zx_weight.reshape(model_width, 2 * inner_width)))
    gate_in = projected[:, :inner_width]
    signal = projected[:, inner_width:]
    states_in = low_back(matmul(seq_rows, bc_weight))
    step_raw = low_back(matmul(seq_rows, dt_weight))
    conv_signal = jax.nn.silu(causal_conv(signal, convx_weight, convx_bias))
    conv_states = jax.nn.silu(causal_conv(states_in, convbc_weight, convbc_bias))
    input_map = low(conv_states[:, :state_size])
    output_map = low(conv_states[:, state_size:])
    step_size = jax.nn.softplus(step_raw + dt_bias)
    log_decay = jnp.cumsum(step_size * -jnp.exp(a_log), axis=0)
    state_match = low_back(matmul(output_map, input_map.T))
    position = jnp.arange(row_count).astype(jnp.int32)
    causal = position[:, None] >= position[None, :]
    spread = log_decay.T[:, :, None] - log_decay.T[:, None, :]
    decay_matrix = jnp.where(causal[None], jnp.exp(jnp.where(causal[None], spread, 0.0)), 0.0)
    mixing = low(state_match[None] * decay_matrix)
    per_head = conv_signal.reshape(row_count, head_count, head_dimension)
    driven = low(per_head * step_size[:, :, None])
    scanned = low_back(contract_heads('hts,shp->thp', mixing, driven))
    joined = scanned + d_skip[None, :, None] * per_head
    gated_out = joined.reshape(row_count, inner_width) * jax.nn.silu(gate_in)
    return (gated_out, lax.optimization_barrier(jnp.sum(gated_out * gated_out, axis=1)))

def mamba_back(gated_out, square_total, norm_gain, out_weight, full_width):
    normed = low(gated_out * lax.rsqrt(square_total[:, None] / full_width + epsilon) * norm_gain)
    return matmul(normed, out_weight)

def attention_part(seq_rows, length, q_weight, kv_weight, o_weight, query_heads, key_heads, head_dimension):
    row_count, model_width = seq_rows.shape
    queries_raw = low_back(matmul(seq_rows, q_weight))
    key_value = low_back(matmul(seq_rows, kv_weight.reshape(model_width, -1)))
    key_width = key_value.shape[1] // 2
    key_rows = low(rotate(key_value[:, :key_width], key_heads, head_dimension))
    value_rows = low(key_value[:, key_width:])
    queries = low(rotate(queries_raw, query_heads, head_dimension))
    group_size = query_heads // key_heads
    query_tensor = queries.reshape(row_count, key_heads, group_size, head_dimension)
    key_tensor = key_rows.reshape(row_count, key_heads, head_dimension)
    value_tensor = value_rows.reshape(row_count, key_heads, head_dimension)
    attention_scores = low_back(contract_heads('ievb,meb->evim', query_tensor, key_tensor) * head_dimension ** (-0.5))
    position = jnp.arange(row_count).astype(jnp.int32)
    allowed = (position[None, :] <= position[:, None]) & (position[None, :] < length)
    masked = jnp.where(allowed, attention_scores, -1e+30)
    largest = lax.optimization_barrier(jnp.max(masked, axis=-1, keepdims=True))
    raised = jnp.exp(masked - largest)
    attention_weights = low(raised / lax.optimization_barrier(jnp.sum(raised, axis=-1, keepdims=True)))
    attended_values = contract_heads('wbql,lwc->qwbc', attention_weights, value_tensor)
    attended_values = low_back(low(attended_values.reshape(row_count, query_heads * head_dimension)))
    return matmul(attended_values, o_weight)

def ffn_part(seq_rows, gu_weight, down_weight):
    model_width = seq_rows.shape[1]
    projected = low_back(matmul(seq_rows, gu_weight.reshape(model_width, -1)))
    hidden_width = projected.shape[1] // 2
    active = low(jax.nn.silu(projected[:, :hidden_width]) * projected[:, hidden_width:])
    return matmul(active, down_weight)

def forward(hidden, seq_lengths, norm1_gain, zx_weight, bc_weight, dt_weight, convx_weight, convx_bias, convbc_weight, convbc_bias, dt_bias, a_log, d_skip, mnorm_gain, mo_weight, q_weight, kv_weight, o_weight, norm2_gain, gu_weight, down_weight):
    normed_one = low(rms_scale(hidden, norm1_gain)).reshape(-1, LEN, D)
    position = jnp.arange(LEN).astype(jnp.int32)

    def mixer_seq(seq_item):
        seq_rows, length = seq_item
        gated_out, squares = mamba_front(seq_rows, zx_weight, bc_weight, dt_weight, convx_weight, convx_bias, convbc_weight, convbc_bias, dt_bias, a_log, d_skip)
        mamba_out = mamba_back(gated_out, squares, mnorm_gain, mo_weight, DI)
        attn_out = attention_part(seq_rows, length, q_weight, kv_weight, o_weight, QH, KVH, HD)
        return (mamba_out + attn_out) * (position < length).astype(jnp.float32)[:, None]
    mixer_out = low_back(lax.map(jax.checkpoint(mixer_seq), (normed_one, seq_lengths)).reshape(-1, D))
    middle = hidden + mixer_out
    normed_two = low(rms_scale(middle, norm2_gain)).reshape(-1, LEN, D)

    def ffn_seq(seq_item):
        seq_rows, length = seq_item
        return ffn_part(seq_rows, gu_weight, down_weight) * (position < length).astype(jnp.float32)[:, None]
    ffn_out = low_back(lax.map(jax.checkpoint(ffn_seq), (normed_two, seq_lengths)).reshape(-1, D))
    return middle + ffn_out

def reference(hidden_in, out_grad, seq_lengths, norm1_gain, zx_weight, bc_weight, dt_weight, convx_weight, convx_bias, convbc_weight, convbc_bias, dt_bias, a_log, d_skip, mnorm_gain, mo_weight, q_weight, kv_weight, o_weight, norm2_gain, gu_weight, down_weight):
    primals = (hidden_in.astype(jnp.float32), norm1_gain.astype(jnp.float32), zx_weight.astype(jnp.float32), bc_weight.astype(jnp.float32), dt_weight.astype(jnp.float32), convx_weight.astype(jnp.float32), convx_bias.astype(jnp.float32), convbc_weight.astype(jnp.float32), convbc_bias.astype(jnp.float32), dt_bias.astype(jnp.float32), a_log.astype(jnp.float32), d_skip.astype(jnp.float32), mnorm_gain.astype(jnp.float32), mo_weight.astype(jnp.float32), q_weight.astype(jnp.float32), kv_weight.astype(jnp.float32), o_weight.astype(jnp.float32), norm2_gain.astype(jnp.float32), gu_weight.astype(jnp.float32), down_weight.astype(jnp.float32))

    def wrapped(hidden, *params):
        return forward(hidden, seq_lengths, *params)
    hidden_out, pullback = jax.vjp(wrapped, *primals)
    grads = pullback(out_grad.astype(jnp.float32))
    return (hidden_out, grads[0], grads[1], grads[2], grads[3], grads[4], grads[5], grads[6], grads[7], grads[8], grads[9], grads[10], grads[11], grads[12], grads[13], grads[14], grads[15], grads[16], grads[17], grads[18], grads[19])
```

```python
import jax
import jax.numpy as jnp
from jax import lax
from jax.sharding import PartitionSpec as P

HD = 64
DI = 1536
BLOCK = 256
BF = jnp.bfloat16
F32 = jnp.float32

epsilon = 1e-05


def mm(left, right):
    return lax.dot_general(left, right, (((1,), (0,)), ((), ())), preferred_element_type=F32)


def mm_nt(left, right):
    return lax.dot_general(left, right, (((1,), (1,)), ((), ())), preferred_element_type=F32)


def mm_tn(left, right):
    return lax.dot_general(left, right, (((0,), (0,)), ((), ())), preferred_element_type=F32)


def heads_dot(form, left, right):
    return jnp.einsum(form, left, right, preferred_element_type=F32)


def after(value, *others):
    return lax.optimization_barrier((value,) + others)[0]


def rms_scale(row_block, gain_vector):
    return (
        row_block
        * lax.rsqrt(jnp.mean(row_block * row_block, axis=-1, keepdims=True) + epsilon)
        * gain_vector
    )


def conv_silu(values, kernel, shift_bias):
    tap_count = kernel.shape[0]
    row_count = values.shape[0]
    padded = jnp.pad(values, ((tap_count - 1, 0), (0, 0)))
    summed = jnp.zeros_like(values) + shift_bias
    for offset in range(tap_count):
        summed = summed + kernel[offset] * padded[offset : offset + row_count]
    return jax.nn.silu(summed)


def running_sum(values):
    row_count, width = values.shape
    size = 128 if row_count % 128 == 0 else row_count
    parts = values.reshape(row_count // size, size, width)
    low_tri = jnp.tril(jnp.ones((size, size), F32))
    inside = jnp.einsum("ij,bjh->bih", low_tri, parts, precision=lax.Precision.HIGHEST)
    count = row_count // size
    strict = jnp.tril(jnp.ones((count, count), F32), -1)
    before = jnp.einsum("cb,bh->ch", strict, inside[:, -1, :], precision=lax.Precision.HIGHEST)
    return (inside + before[:, None, :]).reshape(row_count, width)


def steps(step_raw, dt_bias, a_log):
    step_size = jax.nn.softplus(step_raw + dt_bias)
    return step_size, running_sum(step_size * -jnp.exp(a_log))


def gate_heads(scanned, conv_signal, gate_in, d_skip):
    joined = scanned + jnp.repeat(d_skip, HD)[None, :] * conv_signal
    gated_out = joined * jax.nn.silu(gate_in)
    return gated_out, jnp.sum(gated_out * gated_out, axis=1)


def gated_norm(gated_out, square_total, norm_gain):
    return gated_out * lax.rsqrt(square_total[:, None] / DI + epsilon) * norm_gain


def swiglu(gate_rows, up_rows):
    return jax.nn.silu(gate_rows) * up_rows


def rotate(values, cosine, sine_part):
    row_count, width = values.shape
    half_size = HD // 2
    by_head = values.reshape(row_count, width // HD, HD)
    front_half = by_head[..., :half_size]
    back_half = by_head[..., half_size:]
    turned = jnp.concatenate(
        [front_half * cosine - back_half * sine_part, back_half * cosine + front_half * sine_part],
        axis=-1,
    )
    return turned.reshape(row_count, width)


def split_heads(values):
    return values.reshape(values.shape[0], -1, HD).transpose(1, 0, 2)


def join_heads(values):
    return values.transpose(1, 0, 2).reshape(values.shape[1], -1)


def blocks_of(row_count):
    size = BLOCK if row_count % BLOCK == 0 else row_count
    return [(start, start + size) for start in range(0, row_count, size)]


def stack_blocks(parts, blocks, axis):
    columns = []
    for start, stop in blocks:
        total = None
        for part in parts:
            if part.shape[axis] >= stop:
                piece = lax.slice_in_dim(part, start, stop, axis=axis)
                total = piece if total is None else total + piece
        columns.append(total)
    return jnp.concatenate(columns, axis=axis)


def causal_mask(start, stop):
    return jnp.arange(start, stop)[:, None] >= jnp.arange(stop)[None, :]


def decay_block(decay_heads, start, stop):
    spread = decay_heads[:, start:stop, None] - decay_heads[:, None, :stop]
    return jnp.exp(jnp.where(causal_mask(start, stop)[None], spread, -jnp.inf))


def scan_forward(output_map, input_map, decay_heads, driven):
    blocks = blocks_of(output_map.shape[0])
    mixed, outs = [], []
    for start, stop in blocks:
        match = mm_nt(output_map[start:stop], input_map[:stop])
        mixing = (match[None] * decay_block(decay_heads, start, stop)).astype(BF)
        mixed.append(mixing)
        outs.append(heads_dot("hts,hsp->htp", mixing, driven[:, :stop]))
    return jnp.concatenate(outs, axis=1), mixed


def scan_backward(output_map, input_map, decay_heads, driven, mixed, d_scanned):
    blocks = blocks_of(output_map.shape[0])
    d_driven, d_output, d_input = [], [], []
    for (start, stop), mixing in zip(blocks, mixed):
        cot = d_scanned[:, start:stop]
        d_driven.append(heads_dot("hts,htp->hsp", mixing, cot))
        d_mixing = heads_dot("htp,hsp->hts", cot, driven[:, :stop])
        d_match = jnp.sum(d_mixing * decay_block(decay_heads, start, stop), axis=0).astype(BF)
        d_output.append(mm(d_match, input_map[:stop]))
        d_input.append(mm_tn(d_match, output_map[start:stop]))
    return (
        stack_blocks(d_driven, blocks, 1),
        jnp.concatenate(d_output, axis=0),
        stack_blocks(d_input, blocks, 0),
    )


def attend_forward(queries, keys, values, length):
    blocks = blocks_of(keys.shape[0])
    kept, outs = [], []
    for start, stop in blocks:
        scores = heads_dot("htp,sp->hts", queries[:, start:stop], keys[:stop]) * HD ** (-0.5)
        allowed = causal_mask(start, stop) & (jnp.arange(stop)[None, :] < length)
        masked = jnp.where(allowed[None], scores, -1e30)
        raised = jnp.exp(masked - jnp.max(masked, axis=-1, keepdims=True))
        weights = (raised / jnp.sum(raised, axis=-1, keepdims=True)).astype(BF)
        kept.append(weights)
        outs.append(heads_dot("hts,sp->htp", weights, values[:stop]))
    return jnp.concatenate(outs, axis=1), kept


def attend_backward(queries, keys, values, kept, attended, d_attended):
    blocks = blocks_of(keys.shape[0])
    inner = jnp.sum(attended * d_attended.astype(F32), axis=-1, keepdims=True)
    d_queries, d_keys, d_values = [], [], []
    for (start, stop), weights in zip(blocks, kept):
        cot = d_attended[:, start:stop]
        d_weights = heads_dot("htp,sp->hts", cot, values[:stop])
        d_scores = (weights.astype(F32) * (d_weights - inner[:, start:stop])).astype(BF)
        d_values.append(heads_dot("hts,htp->sp", weights, cot))
        d_queries.append(heads_dot("hts,sp->htp", d_scores, keys[:stop]) * HD ** (-0.5))
        d_keys.append(heads_dot("hts,htp->sp", d_scores, queries[:, start:stop]) * HD ** (-0.5))
    return (
        jnp.concatenate(d_queries, axis=1),
        stack_blocks(d_keys, blocks, 0),
        stack_blocks(d_values, blocks, 0),
    )


def gather_rows(values):
    return lax.all_gather(values.astype(BF), "tensor", axis=0, tiled=True)


def scatter_rows(values):
    return lax.psum_scatter(
        values.astype(BF), "tensor", scatter_dimension=0, tiled=True
    ).astype(F32)


def shards(
    hidden_in,
    out_grad,
    seq_lengths,
    norm1_gain,
    zx_weight,
    bc_weight,
    dt_weight,
    convx_weight,
    convx_bias,
    convbc_weight,
    convbc_bias,
    dt_bias,
    a_log,
    d_skip,
    mnorm_gain,
    mo_weight,
    q_weight,
    kv_weight,
    o_weight,
    norm2_gain,
    gu_weight,
    down_weight,
):
    model_width = hidden_in.shape[1]
    tensor_rank = lax.axis_index("tensor")
    tensor_count = lax.axis_size("tensor")
    inner = zx_weight.shape[2]
    head_count = dt_weight.shape[1]
    q_width = q_weight.shape[1]
    bc_width = bc_weight.shape[1]
    state_size = bc_width // 2
    kv_width = kv_weight.shape[2]
    key_heads = kv_width // HD
    local_heads = q_width // HD
    heads_per_key = local_heads * tensor_count // key_heads
    key_start = (tensor_rank * local_heads // heads_per_key) * HD
    kv_local = lax.dynamic_slice_in_dim(kv_weight, key_start, HD, 2)
    dt_pad = -head_count % 128
    weights_in = jnp.concatenate(
        [
            zx_weight[:, 0],
            zx_weight[:, 1],
            q_weight,
            bc_weight,
            kv_local[:, 0],
            kv_local[:, 1],
            jnp.pad(dt_weight, ((0, 0), (0, dt_pad))),
        ],
        axis=1,
    )
    ends = [inner, 2 * inner, 2 * inner + q_width]
    ends += [ends[2] + bc_width, ends[2] + bc_width + HD, ends[2] + bc_width + 2 * HD]
    gu_flat = jnp.concatenate([gu_weight[:, 0], gu_weight[:, 1]], axis=1)
    ff = gu_weight.shape[2]

    residual = hidden_in.astype(F32)
    normed_one, norm_one_pull = jax.vjp(rms_scale, residual, norm1_gain)
    rows_one = gather_rows(normed_one)
    row_count = rows_one.shape[0]
    length = seq_lengths[0]
    mask = (jnp.arange(row_count) < length)[:, None]
    angles = (
        jnp.arange(row_count, dtype=F32)[:, None]
        * (10000.0 ** (-2.0 * jnp.arange(HD // 2, dtype=F32) / HD))[None, :]
    )
    cosine = jnp.cos(angles)[:, None, :]
    sine_part = jnp.sin(angles)[:, None, :]

    projected = mm(rows_one, weights_in)
    gate_in, signal, q_raw, states_in, key_raw, value_raw, step_pad = jnp.split(
        projected, ends, axis=1
    )
    step_raw = step_pad[:, :head_count]
    conv_signal, signal_pull = jax.vjp(conv_silu, signal, convx_weight, convx_bias)
    conv_states, states_pull = jax.vjp(conv_silu, states_in, convbc_weight, convbc_bias)
    input_map = conv_states[:, :state_size].astype(BF)
    output_map = conv_states[:, state_size:].astype(BF)
    (step_size, log_decay), steps_pull = jax.vjp(steps, step_raw, dt_bias, a_log)
    decay_heads = log_decay.T
    step_wide = jnp.repeat(step_size, HD, axis=1)
    driven_rows = lax.optimization_barrier((conv_signal * step_wide).astype(BF))
    driven = split_heads(driven_rows)
    scanned_heads, mixed = scan_forward(output_map, input_map, decay_heads, driven)
    scanned = join_heads(scanned_heads)
    (gated_out, squares), gate_pull = jax.vjp(gate_heads, scanned, conv_signal, gate_in, d_skip)
    square_total = lax.psum(squares, "tensor")

    queries, rope_q_pull = jax.vjp(lambda v: rotate(v, cosine, sine_part), q_raw)
    key_rows, rope_k_pull = jax.vjp(lambda v: rotate(v, cosine, sine_part), key_raw)
    queries = split_heads(queries.astype(BF))
    key_rows = key_rows.astype(BF)
    value_rows = value_raw.astype(BF)
    attended_heads, kept = attend_forward(queries, key_rows, value_rows, length)
    attended = join_heads(attended_heads).astype(BF)

    normed_gate, gated_pull = jax.vjp(gated_norm, gated_out, square_total, mnorm_gain)
    normed_gate = normed_gate.astype(BF)
    out_parts = jnp.concatenate([normed_gate, attended], axis=1)
    out_weights = jnp.concatenate([mo_weight, o_weight], axis=0)
    partial_mix = jnp.where(mask, mm(out_parts, out_weights), 0.0)
    middle = residual + scatter_rows(partial_mix)
    normed_two, norm_two_pull = jax.vjp(rms_scale, middle, norm2_gain)
    rows_two = gather_rows(normed_two)
    out_cot = jnp.where(mask, gather_rows(out_grad), 0)

    gu_rows = mm(rows_two, gu_flat)
    active, swiglu_pull = jax.vjp(swiglu, gu_rows[:, :ff], gu_rows[:, ff:])
    active = active.astype(BF)
    d_gate_rows, d_up_rows = swiglu_pull(mm_nt(out_cot, down_weight))
    d_gu_rows = jnp.concatenate([d_gate_rows.astype(BF), d_up_rows.astype(BF)], axis=1)
    d_two = scatter_rows(mm_nt(d_gu_rows, gu_flat))
    d_middle_part, d_gain_two = norm_two_pull(d_two)
    d_middle = out_grad.astype(F32) + d_middle_part
    mixer_cot = gather_rows(d_middle)
    partial_ffn = after(jnp.where(mask, mm(active, down_weight), 0.0).astype(BF), mixer_cot)
    hidden_out = middle + scatter_rows(partial_ffn)
    gu_part = after(mm_tn(rows_two, d_gu_rows).astype(BF), mixer_cot)
    down_part = after(mm_tn(active, out_cot).astype(BF), mixer_cot)
    gu_sum, down_sum = lax.psum((gu_part, down_part), "dp")

    mixer_cot = jnp.where(mask, mixer_cot, 0)
    d_out_parts = mm_nt(mixer_cot, out_weights)
    out_part = mm_tn(out_parts, mixer_cot).astype(BF)
    out_sum = lax.psum(after(out_part, gu_sum), "dp")
    d_gated, d_totals, d_mnorm = gated_pull(d_out_parts[:, :inner])
    d_squares = lax.psum(d_totals, "tensor")

    d_attended = split_heads(lax.optimization_barrier(d_out_parts[:, inner:].astype(BF)))
    d_queries, d_keys, d_values = attend_backward(
        queries, key_rows, value_rows, kept, attended_heads, d_attended
    )
    (d_q_raw,) = rope_q_pull(join_heads(d_queries))
    (d_key_raw,) = rope_k_pull(d_keys)

    d_scanned, d_signal_skip, d_gate_in, d_skip_grad = gate_pull((d_gated, d_squares))
    d_scanned = lax.optimization_barrier(d_scanned.astype(BF))
    d_driven_heads, d_output, d_input = scan_backward(
        output_map, input_map, decay_heads, driven, mixed, split_heads(d_scanned)
    )
    d_driven = join_heads(d_driven_heads)
    driven_wide = driven_rows.astype(F32)

    def by_head(values):
        return jnp.sum(values.reshape(row_count, head_count, HD), axis=2)

    d_log_decay = by_head(scanned * d_scanned.astype(F32) - driven_wide * d_driven)
    d_step = by_head(conv_signal * d_driven)
    d_step_raw, d_dt_bias, d_a_log = steps_pull((d_step, d_log_decay))
    d_signal, d_convx, d_convx_bias = signal_pull(d_signal_skip + d_driven * step_wide)
    d_states, d_convbc, d_convbc_bias = states_pull(jnp.concatenate([d_input, d_output], axis=1))

    d_projected = jnp.concatenate(
        [
            d_gate_in.astype(BF),
            d_signal.astype(BF),
            d_q_raw.astype(BF),
            d_states.astype(BF),
            d_key_raw.astype(BF),
            d_values.astype(BF),
            jnp.pad(d_step_raw.astype(BF), ((0, 0), (0, dt_pad))),
        ],
        axis=1,
    )
    d_one = scatter_rows(mm_nt(d_projected, weights_in))
    in_part = mm_tn(rows_one, d_projected)
    kv_part = in_part[:, ends[3] : ends[5]].astype(BF).reshape(model_width, 2, HD)
    kv_placed = lax.dynamic_update_slice_in_dim(
        jnp.zeros(kv_weight.shape, BF), kv_part, key_start, 2
    )
    shared_part = jnp.concatenate(
        [in_part[:, ends[2] : ends[3]].astype(BF), kv_placed[:, 0], kv_placed[:, 1]], axis=1
    )
    split_part = after(in_part[:, : ends[2]].astype(BF), out_sum)
    shared_rows = lax.psum_scatter(shared_part, "tensor", scatter_dimension=0, tiled=True)
    split_sum, shared_rows = lax.psum((split_part, shared_rows), "dp")
    shared_sum = lax.all_gather(shared_rows, "tensor", axis=0, tiled=True).astype(F32)

    d_resid_part, d_gain_one = norm_one_pull(d_one)
    hidden_grad = d_middle + d_resid_part

    own = [
        in_part[:, ends[5] : ends[5] + head_count].T,
        d_convx,
        d_convx_bias,
        d_dt_bias,
        d_a_log,
        d_skip_grad,
        d_mnorm,
    ]
    common = [d_gain_one, d_gain_two, d_convbc, d_convbc_bias]

    def pack(arrays, axes):
        flat = jnp.concatenate([array.reshape(-1) for array in arrays])
        total = lax.psum(flat, axes)
        pieces, start = [], 0
        for array in arrays:
            pieces.append(total[start : start + array.size].reshape(array.shape))
            start += array.size
        return pieces

    dt_sum, convx_sum, convx_bias_sum, dt_bias_sum, a_log_sum, skip_sum, mnorm_sum = pack(
        own, "dp"
    )
    gain_one_sum, gain_two_sum, convbc_sum, convbc_bias_sum = pack(common, ("dp", "tensor"))

    split_sum = split_sum.astype(F32)
    out_sum = out_sum.astype(F32)
    gu_sum = gu_sum.astype(F32)
    return (
        hidden_out,
        hidden_grad,
        gain_one_sum,
        jnp.stack([split_sum[:, :inner], split_sum[:, inner : 2 * inner]], axis=1),
        shared_sum[:, :bc_width],
        dt_sum.T,
        convx_sum,
        convx_bias_sum,
        convbc_sum,
        convbc_bias_sum,
        dt_bias_sum,
        a_log_sum,
        skip_sum,
        mnorm_sum,
        out_sum[:inner],
        split_sum[:, 2 * inner :],
        jnp.stack(
            [shared_sum[:, bc_width : bc_width + kv_width], shared_sum[:, bc_width + kv_width :]],
            axis=1,
        ),
        out_sum[inner:],
        gain_two_sum,
        jnp.stack([gu_sum[:, :ff], gu_sum[:, ff:]], axis=1),
        down_sum.astype(F32),
    )


def solution(mesh):
    return jax.shard_map(
        shards,
        mesh=mesh,
        in_specs=(
            P(("dp", "tensor"), None),
            P(("dp", "tensor"), None),
            P("dp"),
            P(),
            P(None, None, "tensor"),
            P(),
            P(None, "tensor"),
            P(None, "tensor"),
            P("tensor"),
            P(),
            P(),
            P("tensor"),
            P("tensor"),
            P("tensor"),
            P("tensor"),
            P("tensor", None),
            P(None, "tensor"),
            P(),
            P("tensor", None),
            P(),
            P(None, None, "tensor"),
            P("tensor", None),
        ),
        out_specs=(
            P(("dp", "tensor"), None),
            P(("dp", "tensor"), None),
            P(),
            P(None, None, "tensor"),
            P(),
            P(None, "tensor"),
            P(None, "tensor"),
            P("tensor"),
            P(),
            P(),
            P("tensor"),
            P("tensor"),
            P("tensor"),
            P("tensor"),
            P("tensor", None),
            P(None, "tensor"),
            P(),
            P("tensor", None),
            P(),
            P(None, None, "tensor"),
            P("tensor", None),
        ),
        check_vma=False,
    )
```
